32 devices in a mesh: band: 4 (over y, x), dom: 8 (over z, core).
Axes of the slice: x: 2, y: 2, z: 4, core: 2. Of those that a mesh axis runs over, the one named last changes fastest.
Arguments:
- wave: bfloat16 [48, 19, 13, 1024], P('dom', None, None, 'band'), parts along dimension 3, may hold values from -6 to 6
- kinetic: bfloat16 [343, 343], replicated, may hold values from -1 to 1, as said below
- cell_scale: float32 [48], P('dom'), may hold values from 0.5 to 2
- potential: float32 [48, 19, 13], P('dom'), may hold values from 0.2 to 2
- proj_values: bfloat16 [128, 343], P('dom'), may hold values from -0.23925781 to 0.23925781
- piece_cell: int32 [128], P('dom'), may hold values from 0 to 5
- piece_proj: int32 [128], P('dom'), may hold values from 0 to 255
- coupling: float32 [256], replicated, may hold values from 0.5 to 2
- center: float32 [1], replicated, may hold values from 9 to 11
- halfwidth: float32 [1], replicated, may hold values from 14 to 18
Outputs:
- filtered: float32 [48, 19, 13, 1024], P('dom', None, None, 'band'), parts along dimension 3
The draws below stay inside these ranges and needn't reach their ends.
There are 4 independent parts, one for each index of `band`. The reference program is written for one: setup_inputs(seed, part) draws one part's arguments, and reference() takes and returns one part's arrays. A program takes and returns all parts, laid end to end along the dimension named above; an argument that names none is the same for every part. Nothing has to cross between parts.
Inputs may be any that keep to these rules, and one draw needn't show every extreme that they name: kinetic is symmetric.
All inputs are finite; a program needn't handle non-finite values.
Results may differ from the reference program's by a relative error of at most 0.0014.
Values may be sent and summed in bfloat16 or wider, within the bound.
A program may use at most 64 MiB of HBM per device.

```python
import math
import jax
import jax.numpy as jnp
from jax import lax

P_SIZE = 7
NC = 343
CXC = 2
CYC = 3
CZC = 1
CELLS_DEV = 6
CELLS = 48
ZL = 6
ZN = 48
NYN = 19
NXN = 13
BLOCK = 128
COLS = 256
NPROJ = 256
PIECES_DEV = 16
PIECES = 128
DEGREE = 4
N_DOM = 8


def draw_kinetic(key, part):
    key_off = jax.random.fold_in(key, 11)
    key_diag = jax.random.fold_in(key, 12)
    noise_draw = jax.random.normal(key_off, (NC, NC), jnp.float32)
    symmetric = (noise_draw + noise_draw.T) * (0.02 / 1.4142135)
    diag_vals = jax.random.uniform(key_diag, (NC,), jnp.float32, minval=0.5, maxval=1.0)
    identity = jnp.eye(NC, dtype=jnp.float32)
    return (symmetric * (1.0 - identity) + identity * diag_vals[None, :]).astype(jnp.bfloat16)


def set_ends(drawn, stream_key, smallest, largest):
    spot = [jax.random.randint(jax.random.fold_in(stream_key, axis), (), 0, length) for axis, length in enumerate(drawn.shape)]
    longest = drawn.shape.index(max(drawn.shape))
    neighbour = spot[:longest] + [(spot[longest] + 1) % drawn.shape[longest]] + spot[longest + 1:]
    return drawn.at[tuple(spot)].set(smallest).at[tuple(neighbour)].set(largest)


def shard_levels(key, dims, split, low, high):
    def one(axis_at, parts):
        draws = jax.random.uniform(jax.random.fold_in(jax.random.fold_in(key, 6), axis_at), (parts,), jnp.float32, low / len(split), high / len(split))
        return jnp.repeat(jnp.exp(draws), dims[axis_at] // parts).reshape((-1,) + (1,) * (len(dims) - axis_at - 1))

    loudness = one(*split[0])
    for cut in split[1:]:
        loudness = loudness * one(*cut)
    return loudness


def noise(stream_key, extent, deviation, most, split=(), kind=jnp.bfloat16):
    values = deviation * jax.random.normal(stream_key, extent, jnp.float32)
    if split:
        values = values * shard_levels(stream_key, extent, split, -0.22, 0.18)
    return jnp.clip(values, -most, most).astype(kind)


def setup_inputs(seed: int = 0, part: int = 0) -> dict:
    streams_of = jax.random.split(jax.random.key(seed), 11)
    part_splits = jax.random.split(jax.random.fold_in(streams_of[10], part), 11)
    return {
        "wave": noise(part_splits[0], (ZN, NYN, NXN, COLS), 1.0, 6.0, ((0, 8),)),
        "kinetic": draw_kinetic(jax.random.fold_in(streams_of[10], 71), part),
        "cell_scale": jnp.clip(jnp.exp(math.log(2.0) - 1.3862944 * jax.random.uniform(streams_of[2], (CELLS,), jnp.float32) ** shard_levels(streams_of[2], (CELLS,), ((0, 8),), -0.2, 0.2)), 0.5, 2.0),
        "potential": jnp.clip(0.2 + 1.8 * jax.random.uniform(streams_of[3], (ZN, NYN, NXN), jnp.float32) ** shard_levels(streams_of[3], (ZN, NYN, NXN), ((0, 8),), -0.2, 0.2), 0.2, 2.0),
        "proj_values": noise(streams_of[4], (PIECES, NC), 0.04, 0.23925781, ((0, 8),)),
        "piece_cell": set_ends(jax.random.randint(streams_of[5], (PIECES,), 0, CELLS_DEV), jax.random.fold_in(streams_of[5], 1), 0, CELLS_DEV - 1).astype(jnp.int32),
        "piece_proj": set_ends(jax.random.randint(streams_of[6], (PIECES,), 0, NPROJ), jax.random.fold_in(streams_of[6], 1), 0, NPROJ - 1).astype(jnp.int32),
        "coupling": jnp.clip(jnp.exp(jax.random.uniform(streams_of[7], (NPROJ,), jnp.float32, math.log(0.5), math.log(2.0))), 0.5, 2.0),
        "center": jnp.clip(jax.random.uniform(streams_of[8], (1,), jnp.float32, 9.0, 11.0), 9.0, 11.0),
        "halfwidth": jnp.clip(jax.random.uniform(streams_of[9], (1,), jnp.float32, 14.0, 18.0), 14.0, 18.0),
    }


def selector(count, total_nodes):
    row_ids = jnp.arange(count * P_SIZE, dtype=jnp.int32)
    target = (row_ids // P_SIZE) * (P_SIZE - 1) + row_ids % P_SIZE
    node_ids = jnp.arange(total_nodes, dtype=jnp.int32)
    return (target[:, None] == node_ids[None, :]).astype(jnp.float32)


def extract(extended):
    pick_z = selector(CZC, extended.shape[0])
    pick_y = selector(CYC, extended.shape[1])
    pick_x = selector(CXC, extended.shape[2])
    width = extended.shape[3]
    gathered = jnp.einsum('zyxk,az,by,cx->abck', extended.astype(jnp.float32), pick_z, pick_y, pick_x,
                          precision=lax.Precision.HIGHEST)
    gathered = gathered.reshape(CZC, P_SIZE, CYC, P_SIZE, CXC, P_SIZE, width).transpose(0, 2, 4, 1, 3, 5, 6)
    return gathered.reshape(CZC * CYC * CXC, P_SIZE * P_SIZE * P_SIZE, width).astype(jnp.bfloat16)


def assemble(cell_out):
    width = cell_out.shape[2]
    grouped = cell_out.reshape(CZC, CYC, CXC, P_SIZE, P_SIZE, P_SIZE, width).transpose(0, 3, 1, 4, 2, 5, 6)
    grouped = grouped.reshape(CZC * P_SIZE, CYC * P_SIZE, CXC * P_SIZE, width)
    pick_z = selector(CZC, ZL + 1)
    pick_y = selector(CYC, NYN)
    pick_x = selector(CXC, NXN)
    return jnp.einsum('abck,az,by,cx->zyxk', grouped, pick_z, pick_y, pick_x, precision=lax.Precision.HIGHEST)


def domain_cells(rounded, domain):
    owned = lax.dynamic_slice_in_dim(rounded, (domain * ZL).astype(jnp.int32), ZL, 0)
    following = lax.dynamic_slice_in_dim(rounded, (((domain + 1) % N_DOM) * ZL).astype(jnp.int32), 1, 0)
    return extract(jnp.concatenate([owned, following], axis=0))


def apply_hamiltonian(current, kinetic, cell_scale, potential, proj_values, piece_cell, piece_proj, coupling,
                      center, halfwidth):
    width = current.shape[3]
    rounded = current.astype(jnp.bfloat16)
    domains = jnp.arange(N_DOM, dtype=jnp.int32)
    values_dom = proj_values.reshape(N_DOM, PIECES_DEV, P_SIZE * P_SIZE * P_SIZE)
    cells_dom = piece_cell.reshape(N_DOM, PIECES_DEV)
    projs_dom = piece_proj.reshape(N_DOM, PIECES_DEV)
    scales_dom = cell_scale.reshape(N_DOM, CELLS_DEV)
    proj_ids = jnp.arange(NPROJ, dtype=jnp.int32)

    def coefficient_part(items):
        domain, cell_idx, proj_idx, values = items
        cell_vals = domain_cells(rounded, domain)
        picked = jnp.take(cell_vals, cell_idx, axis=0)
        piece_coef = jnp.einsum('np,npk->nk', values.astype(jnp.float32), picked.astype(jnp.float32),
                                precision=lax.Precision.HIGHEST)
        proj_hot = (proj_idx[None, :] == proj_ids[:, None]).astype(jnp.float32)
        return jnp.dot(proj_hot, piece_coef, precision=lax.Precision.HIGHEST)

    partials = lax.map(coefficient_part, (domains, cells_dom, projs_dom, values_dom))
    summed = jnp.sum(partials, axis=0)
    scaled = (coupling[:, None] * summed).astype(jnp.bfloat16)

    def cell_part(items):
        domain, cell_idx, proj_idx, values, scales = items
        cell_vals = domain_cells(rounded, domain)
        cell_out = jnp.einsum('pq,nqk->npk', kinetic.astype(jnp.float32), cell_vals.astype(jnp.float32),
                              precision=lax.Precision.HIGHEST) * scales[:, None, None]
        proj_hot = (proj_idx[None, :] == proj_ids[:, None]).astype(jnp.float32)
        per_piece = jnp.dot(proj_hot.T, scaled.astype(jnp.float32), precision=lax.Precision.HIGHEST)
        weighted = values.astype(jnp.float32)[:, :, None] * per_piece[:, None, :]
        cell_hot = (cell_idx[None, :] == jnp.arange(CELLS_DEV, dtype=jnp.int32)[:, None]).astype(jnp.float32)
        cell_out = cell_out + jnp.einsum('mn,npk->mpk', cell_hot, weighted, precision=lax.Precision.HIGHEST)
        return assemble(cell_out)

    pieces = lax.map(cell_part, (domains, cells_dom, projs_dom, values_dom, scales_dom))
    layers = pieces[:, :ZL]
    tops = pieces[:, ZL]
    layers = layers.at[:, 0].add(jnp.roll(tops, 1, axis=0))
    applied = layers.reshape(ZN, NYN, NXN, width)
    return (applied + (potential[..., None] - center[0]) * current) / halfwidth[0]


def filter_block(block, operands):
    previous = block.astype(jnp.float32)
    current = apply_hamiltonian(previous, *operands)
    for step in range(DEGREE - 1):
        following = 2.0 * apply_hamiltonian(current, *operands) - previous
        previous = current
        current = following
    return current


def reference(wave, kinetic, cell_scale, potential, proj_values, piece_cell, piece_proj, coupling, center,
              halfwidth):
    operands = (kinetic, cell_scale, potential, proj_values, piece_cell, piece_proj, coupling, center, halfwidth)
    first = filter_block(wave[..., :BLOCK], operands)
    second = filter_block(wave[..., BLOCK:], operands)
    return jnp.concatenate([first, second], axis=3)
```

```python
import functools

import jax
import jax.numpy as jnp
from jax import lax
from jax.experimental import pallas as pl
from jax.experimental.pallas import tpu as pltpu
from jax.sharding import PartitionSpec as P

ZL = 6
NL = 7
LINES = 19
NXN = 13
ROWS = LINES * 8
KROWS = 160
KDIM = NL * 64
PIECES = 16
STEPS = 4
F32 = jnp.float32
BF16 = jnp.bfloat16


def dot(a, b):
    return jnp.dot(a, b, preferred_element_type=F32)


def joined(first, second):
    row = lax.broadcasted_iota(jnp.int32, first.shape, 1)
    moved_second = pltpu.roll(second, 6, 1)
    moved_first = pltpu.roll(first, 2, 1)
    return (
        first + jnp.where(row == 6, moved_second, 0.0),
        second + jnp.where(row == 0, moved_first, 0.0),
    )


def wave_lines(layer):
    layer = layer.astype(F32)
    empty = jnp.zeros((LINES, 1, layer.shape[2]), F32)
    return layer[:, 0:8], jnp.concatenate([layer[:, 6:NXN], empty], axis=1)


def kernel(
    n, scale, pc, pp, center, hw, wave, kin, pot, pv, coup, out,
    Y, Vb, G, L1, L2, U, M, acc, pot6, pvx, meta, ini_s, ini_r,
    up_s, up_r, dn_s, dn_r, coef, cpl,
    meta_ss, meta_rs, set_ss, set_rs, coef_ss, coef_rs, pl_ss, pl_rs,
):
    me = lax.axis_index("dom")
    cols = wave.shape[3]

    def to(offset):
        return {"dom": lax.rem(me + offset, n)}

    def copy(src, dst, ss, rs, offset):
        return pltpu.make_async_remote_copy(
            src_ref=src, dst_ref=dst, send_sem=ss, recv_sem=rs,
            device_id=to(offset), device_id_type=pl.DeviceIdType.MESH,
        )

    barrier = pltpu.get_barrier_semaphore()
    for r in range(1, n):
        pl.semaphore_signal(barrier, inc=1, device_id=to(r), device_id_type=pl.DeviceIdType.MESH)

    first, second = wave_lines(wave[0])
    ini_s[...] = jnp.concatenate([first, second], axis=1).astype(BF16).reshape(LINES * 16, cols)
    row = lax.broadcasted_iota(jnp.int32, (PIECES, 128), 0)
    lane = lax.broadcasted_iota(jnp.int32, (PIECES, 128), 1)
    table = jnp.zeros((PIECES, 128), jnp.int32)
    for i in range(PIECES):
        table = jnp.where(row == i, jnp.where(lane < 64, pp[i], pc[i]), table)
    meta[0] = table.astype(F32)

    pl.semaphore_wait(barrier, n - 1)
    setup = [
        copy(ini_s, ini_r, set_ss.at[0], set_rs.at[0], n - 1),
        copy(pot.at[0], pot6, set_ss.at[1], set_rs.at[1], n - 1),
        copy(pv, pvx.at[0], set_ss.at[2], set_rs.at[2], n - 1),
        copy(pv, pvx.at[1], set_ss.at[3], set_rs.at[3], 1),
    ]
    for c in setup:
        c.start()
    metas = [copy(meta.at[0], meta.at[r], meta_ss.at[r], meta_rs.at[r], r) for r in range(1, n)]
    for c in metas:
        c.start()

    def place(index):
        a, b, c = index // 64, (index // 8) % 8, index % 8
        return jnp.where((b < 7) & (c < 7), a * 49 + b * 7 + c, -1)

    nodes = kin.shape[0]
    spread = (
        lax.broadcasted_iota(jnp.int32, (nodes, KDIM), 0)
        == place(lax.broadcasted_iota(jnp.int32, (1, KDIM), 1))
    ).astype(F32).astype(BF16)
    spread_t = (
        lax.broadcasted_iota(jnp.int32, (KDIM, nodes), 1)
        == place(lax.broadcasted_iota(jnp.int32, (KDIM, 1), 0))
    ).astype(F32).astype(BF16)
    full = dot(spread_t, dot(kin[...], spread).astype(BF16))
    ends = jnp.concatenate([full[0:56], full[384:440]], axis=0)
    inner = [full[64 * a : 64 * a + 56] for a in range(1, ZL)]
    L2[...] = jnp.concatenate(inner + [jnp.zeros((8, KDIM), F32)], axis=0).astype(BF16)
    own = dot(pv[...], spread)
    own_cell = meta[0][:, 64:65]
    for cell in range(6):
        L1[cell] = jnp.concatenate([jnp.where(own_cell == float(cell), own, 0.0), ends], axis=0).astype(BF16)

    inv = 1.0 / hw[0]

    def put_shift(a, layer):
        wide = jnp.broadcast_to(layer[:, None, :], (LINES, 8, NXN))
        for cx in range(2):
            pick = (
                lax.broadcasted_iota(jnp.int32, wide.shape, 2)
                == lax.broadcasted_iota(jnp.int32, wide.shape, 1) + 6 * cx
            )
            value = jnp.sum(jnp.where(pick, wide, 0.0), axis=2, keepdims=True)
            value = jnp.broadcast_to((value - center[0]) * inv, (LINES, 8, 128))
            G[cx, a] = value.reshape(ROWS, 128)

    def put_start(a, pair):
        for cx in range(2):
            flat = pair[cx].reshape(ROWS, cols)
            Y[0, cx, a] = flat
            Y[1, cx, a] = jnp.zeros((ROWS, cols), F32)
            put_operand(cx, a, flat)

    def put_operand(cx, a, flat):
        Vb[cx, a] = jnp.concatenate([flat, jnp.zeros((8, cols), F32)], axis=0).astype(BF16)

    for a in range(ZL):
        put_start(a, wave_lines(wave[a]))
        put_shift(a, pot[a])

    for c in setup + metas:
        c.wait_recv()
    arrived = ini_r[...].astype(F32).reshape(LINES, 16, cols)
    put_start(ZL, (arrived[:, 0:8], arrived[:, 8:16]))
    put_shift(ZL, pot6[...])

    values = jnp.concatenate([pv[...], pvx[0], pvx[1]], axis=0).astype(F32)
    table = jnp.concatenate([meta[0], meta[n - 1], meta[1]], axis=0)
    cells = table[:, 64:65]
    group = lax.broadcasted_iota(jnp.int32, (56, 3 * PIECES), 1)
    parts = []
    for cell in range(6):
        masked = jnp.where(cells == float(cell), values, 0.0).astype(BF16)
        base = lax.dot_general(spread_t, masked, (((1,), (1,)), ((), ())), preferred_element_type=F32)
        low, high = base[0:56], base[384:440]
        layers = []
        for a in range(NL):
            here = jnp.where(group < PIECES, base[64 * a : 64 * a + 56], 0.0)
            if a == 0:
                here = here + jnp.where(group >= 2 * PIECES, high, 0.0)
            if a == ZL:
                here = here + jnp.where((group >= PIECES) & (group < 2 * PIECES), low, 0.0)
            layers.append(here)
        parts.append(layers)
    for a in range(NL):
        pair = []
        for cx in range(2):
            c0, c1, c2 = (parts[2 * cy + cx][a] for cy in range(3))
            whole = jnp.concatenate(
                [c0[0:48], c0[48:56] + c1[0:8], c1[8:48], c1[48:56] + c2[0:8], c2[8:56]], axis=0
            )
            pair.append(whole.reshape(LINES, 8, 3 * PIECES))
        for cx, whole in enumerate(joined(*pair)):
            flat = whole.reshape(ROWS, 3 * PIECES)
            U[cx, a] = jnp.concatenate([flat, jnp.zeros((8, 3 * PIECES), F32)], axis=0).astype(BF16)

    count = coup.shape[1]
    number = lax.broadcasted_iota(jnp.int32, (1, count), 1).astype(F32)
    hot = jnp.where(table[:, 0:1] == number, 1.0, 0.0)
    every = jnp.where(meta[...].reshape(n * PIECES, 128)[:, 0:1] == number, 1.0, 0.0).astype(BF16)
    M[...] = lax.dot_general(
        hot.astype(BF16), every, (((1,), (1,)), ((), ())), preferred_element_type=F32
    ).astype(BF16)
    cpl[...] = jnp.broadcast_to(
        jnp.sum(hot * coup[...], axis=1, keepdims=True), (3 * PIECES, cols)
    )

    def add_cell(cx, cy, a, part):
        if cy == 0:
            acc[cx, a, 0:56] = part
        else:
            acc[cx, a, 48 * cy : 48 * cy + 8] += part[0:8]
            acc[cx, a, 48 * cy + 8 : 48 * cy + 56] = part[8:56]

    def both(a):
        return joined(
            acc[0, a].reshape(LINES, 8, cols), acc[1, a].reshape(LINES, 8, cols)
        )

    def step(k, last):
        cur = lax.rem(k, 2)
        other = 1 - cur
        is_first = (k == 0) if isinstance(k, int) else None
        if is_first is None:
            factor = jnp.where(k == 0, 1.0, 2.0)
            back = jnp.where(k == 0, 0.0, 1.0)
        else:
            factor = 1.0 if is_first else 2.0
            back = 0.0 if is_first else 1.0
        gain = factor * inv

        def operand(cx, cy):
            return Vb[cx, :, 48 * cy : 48 * cy + 64, :].reshape(KDIM, cols)

        total = jnp.zeros((PIECES, cols), F32)
        for cy in range(3):
            for cx in range(2):
                cell = 2 * cy + cx
                result = dot(L1[cell], operand(cx, cy))
                total = total + result[0:PIECES]
                factor_c = scale[cell]
                add_cell(cx, cy, 0, result[16:72] * factor_c)
                add_cell(cx, cy, ZL, result[72:128] * factor_c)
        coef[k, 0] = total.astype(BF16)
        coefs = [
            copy(coef.at[k, 0], coef.at[k, r], coef_ss.at[k, r], coef_rs.at[k, r], r) for r in range(1, n)
        ]
        for c in coefs:
            c.start()
        planes = []
        ends = [ZL] if last else [ZL, 0]
        for a in ends:
            pair = both(a)
            packed = jnp.concatenate(pair, axis=1).astype(BF16).reshape(LINES * 16, cols)
            if a == ZL:
                up_s[k] = packed
                c = copy(up_s.at[k], up_r.at[k], pl_ss.at[k, 0], pl_rs.at[k, 0], 1)
            else:
                dn_s[k] = packed
                c = copy(dn_s.at[k], dn_r.at[k], pl_ss.at[k, 1], pl_rs.at[k, 1], n - 1)
            c.start()
            planes.append(c)

        for cy in range(3):
            for cx in range(2):
                result = dot(L2[...], operand(cx, cy)) * scale[2 * cy + cx]
                for a in range(1, ZL):
                    add_cell(cx, cy, a, result[56 * (a - 1) : 56 * a])

        def partial(a):
            for cx, whole in enumerate(both(a)):
                shift = G[cx, a] * factor
                shift = jnp.concatenate([shift] * (cols // 128), axis=1)
                Y[other, cx, a] = (
                    whole.reshape(ROWS, cols) * gain + shift * Y[cur, cx, a] - back * Y[other, cx, a]
                )

        for a in range(ZL if last else NL):
            partial(a)

        for c in coefs:
            c.wait_recv()
        scaled = dot(M[...], coef[k].reshape(n * PIECES, cols)) * cpl[...]
        scaled = scaled.astype(BF16)

        def finish(a, extra):
            pair = []
            for cx in range(2):
                far = dot(U[cx, a], scaled)[0:ROWS]
                if extra is not None:
                    far = far + extra[cx].reshape(ROWS, cols)
                new = Y[other, cx, a] + gain * far
                if last:
                    pair.append(new.reshape(LINES, 8, cols))
                else:
                    Y[other, cx, a] = new
                    put_operand(cx, a, new)
            if last:
                out[a] = jnp.concatenate([pair[0][:, 0:7], pair[1][:, 1:7]], axis=1)

        for a in range(1, ZL):
            finish(a, None)
        for c in planes:
            c.wait_recv()
        got = up_r[k].astype(F32).reshape(LINES, 16, cols)
        finish(0, (got[:, 0:8], got[:, 8:16]))
        if not last:
            got = dn_r[k].astype(F32).reshape(LINES, 16, cols)
            finish(ZL, (got[:, 0:8], got[:, 8:16]))
        for c in coefs + planes:
            c.wait_send()

    @pl.loop(0, STEPS - 1)
    def _(k):
        step(k, False)

    step(STEPS - 1, True)
    for c in setup + metas:
        c.wait_send()


def local(n, wave, kinetic, cell_scale, potential, proj_values, piece_cell, piece_proj, coupling, center, halfwidth):
    cols = wave.shape[3]
    plane = (LINES * 16, cols)
    smem = pl.BlockSpec(memory_space=pltpu.SMEM)
    vmem = pl.BlockSpec(memory_space=pltpu.VMEM)
    dma = pltpu.SemaphoreType.DMA
    return pl.pallas_call(
        functools.partial(kernel, n),
        out_shape=jax.ShapeDtypeStruct(wave.shape, F32),
        in_specs=[smem] * 5 + [vmem] * 5,
        out_specs=vmem,
        scratch_shapes=[
            pltpu.VMEM((2, 2, NL, ROWS, cols), F32),
            pltpu.VMEM((2, NL, KROWS, cols), BF16),
            pltpu.VMEM((2, NL, ROWS, 128), F32),
            pltpu.VMEM((6, 128, KDIM), BF16),
            pltpu.VMEM((288, KDIM), BF16),
            pltpu.VMEM((2, NL, KROWS, 3 * PIECES), BF16),
            pltpu.VMEM((3 * PIECES, n * PIECES), BF16),
            pltpu.VMEM((2, NL, ROWS, cols), F32),
            pltpu.VMEM((LINES, NXN), F32),
            pltpu.VMEM((2,) + proj_values.shape, BF16),
            pltpu.VMEM((n, PIECES, 128), F32),
            pltpu.VMEM(plane, BF16),
            pltpu.VMEM(plane, BF16),
            pltpu.VMEM((STEPS,) + plane, BF16),
            pltpu.VMEM((STEPS,) + plane, BF16),
            pltpu.VMEM((STEPS - 1,) + plane, BF16),
            pltpu.VMEM((STEPS - 1,) + plane, BF16),
            pltpu.VMEM((STEPS, n, PIECES, cols), BF16),
            pltpu.VMEM((3 * PIECES, cols), F32),
            dma((n,)), dma((n,)), dma((4,)), dma((4,)),
            dma((STEPS, n)), dma((STEPS, n)), dma((STEPS, 2)), dma((STEPS, 2)),
        ],
        compiler_params=pltpu.CompilerParams(
            collective_id=0, has_side_effects=True, vmem_limit_bytes=48 * 1024 * 1024
        ),
        name="filter",
    )(
        cell_scale, piece_cell, piece_proj, center, halfwidth,
        wave, kinetic, potential, proj_values, coupling[None, :],
    )


def solution(mesh):
    in_specs = (
        P("dom", None, None, "band"), P(), P("dom"), P("dom", None, None), P("dom", None),
        P("dom"), P("dom"), P(), P(), P(),
    )
    return jax.shard_map(
        functools.partial(local, mesh.shape["dom"]), mesh=mesh, in_specs=in_specs,
        out_specs=P("dom", None, None, "band"), check_vma=False,
    )
```

```python
import functools

import jax
import jax.numpy as jnp
from jax import lax
from jax.experimental import pallas as pl
from jax.experimental.pallas import tpu as pltpu
from jax.sharding import PartitionSpec as P

ZL = 6
NL = 7
LINES = 19
NXN = 13
ROWS = LINES * 8
KROWS = 160
KDIM = NL * 64
PIECES = 16
STEPS = 4
F32 = jnp.float32
BF16 = jnp.bfloat16


def dot(a, b):
    return jnp.dot(a, b, preferred_element_type=F32)


def joined(first, second):
    row = lax.broadcasted_iota(jnp.int32, first.shape, 1)
    moved_second = pltpu.roll(second, 6, 1)
    moved_first = pltpu.roll(first, 2, 1)
    return (
        first + jnp.where(row == 6, moved_second, 0.0),
        second + jnp.where(row == 0, moved_first, 0.0),
    )


def wave_lines(layer):
    layer = layer.astype(F32)
    empty = jnp.zeros((LINES, 1, layer.shape[2]), F32)
    return layer[:, 0:8], jnp.concatenate([layer[:, 6:NXN], empty], axis=1)


def kernel(
    n, scale, pc, pp, center, hw, wave_hbm, kin_hbm, pot_hbm, pv_hbm, coup, out,
    wave, kin, pot, pv, in_sem,
    Y, Vb, G, L1, L2, U, M, acc, pot6, pvx, meta, ini_s, ini_r,
    up_s, up_r, dn_s, dn_r, coef, cpl,
    meta_ss, meta_rs, set_ss, set_rs, coef_ss, coef_rs, pl_ss, pl_rs,
):
    me = lax.axis_index("dom")
    cols = wave.shape[3]
    loads = [
        pltpu.make_async_copy(wave_hbm.at[0], wave.at[0], in_sem.at[0]),
        pltpu.make_async_copy(pot_hbm, pot, in_sem.at[1]),
        pltpu.make_async_copy(pv_hbm, pv, in_sem.at[2]),
        pltpu.make_async_copy(kin_hbm, kin, in_sem.at[3]),
        pltpu.make_async_copy(wave_hbm.at[1:ZL], wave.at[1:ZL], in_sem.at[4]),
    ]
    for c in loads:
        c.start()

    def to(offset):
        return {"dom": lax.rem(me + offset, n)}

    def copy(src, dst, ss, rs, offset):
        return pltpu.make_async_remote_copy(
            src_ref=src, dst_ref=dst, send_sem=ss, recv_sem=rs,
            device_id=to(offset), device_id_type=pl.DeviceIdType.MESH,
        )

    barrier = pltpu.get_barrier_semaphore()
    for r in range(1, n):
        pl.semaphore_signal(barrier, inc=1, device_id=to(r), device_id_type=pl.DeviceIdType.MESH)

    loads[0].wait()
    first, second = wave_lines(wave[0])
    ini_s[...] = jnp.concatenate([first, second], axis=1).astype(BF16).reshape(LINES * 16, cols)
    row = lax.broadcasted_iota(jnp.int32, (PIECES, 128), 0)
    lane = lax.broadcasted_iota(jnp.int32, (PIECES, 128), 1)
    table = jnp.zeros((PIECES, 128), jnp.int32)
    for i in range(PIECES):
        table = jnp.where(row == i, jnp.where(lane < 64, pp[i], pc[i]), table)
    meta[0] = table.astype(F32)

    loads[1].wait()
    loads[2].wait()
    pl.semaphore_wait(barrier, n - 1)
    setup = [
        copy(ini_s, ini_r, set_ss.at[0], set_rs.at[0], n - 1),
        copy(pot.at[0], pot6, set_ss.at[1], set_rs.at[1], n - 1),
        copy(pv, pvx.at[0], set_ss.at[2], set_rs.at[2], n - 1),
        copy(pv, pvx.at[1], set_ss.at[3], set_rs.at[3], 1),
    ]
    for c in setup:
        c.start()
    metas = [copy(meta.at[0], meta.at[r], meta_ss.at[r], meta_rs.at[r], r) for r in range(1, n)]
    for c in metas:
        c.start()

    def place(index):
        a, b, c = index // 64, (index // 8) % 8, index % 8
        return jnp.where((b < 7) & (c < 7), a * 49 + b * 7 + c, -1)

    loads[3].wait()
    nodes = kin.shape[0]
    spread = (
        lax.broadcasted_iota(jnp.int32, (nodes, KDIM), 0)
        == place(lax.broadcasted_iota(jnp.int32, (1, KDIM), 1))
    ).astype(F32).astype(BF16)
    spread_t = (
        lax.broadcasted_iota(jnp.int32, (KDIM, nodes), 1)
        == place(lax.broadcasted_iota(jnp.int32, (KDIM, 1), 0))
    ).astype(F32).astype(BF16)
    full = dot(spread_t, dot(kin[...], spread).astype(BF16))
    ends = jnp.concatenate([full[0:56], full[384:440]], axis=0)
    inner = [full[64 * a : 64 * a + 56] for a in range(1, ZL)]
    L2[...] = jnp.concatenate(inner + [jnp.zeros((8, KDIM), F32)], axis=0).astype(BF16)
    own = dot(pv[...], spread)
    own_cell = meta[0][:, 64:65]
    for cell in range(6):
        L1[cell] = jnp.concatenate([jnp.where(own_cell == float(cell), own, 0.0), ends], axis=0).astype(BF16)

    inv = 1.0 / hw[0]

    def put_shift(a, layer):
        layer = (layer - center[0]) * inv
        layer = jnp.concatenate([layer, jnp.zeros((3, LINES), F32)], axis=0)
        halves = (layer[0:8], pltpu.roll(layer, 10, 0)[0:8])
        for cx in range(2):
            for line in range(LINES):
                column = halves[cx][:, line : line + 1]
                G[cx, a, 8 * line : 8 * line + 8] = jnp.broadcast_to(column, (8, 128))

    def put_start(a, pair):
        for cx in range(2):
            flat = pair[cx].reshape(ROWS, cols)
            Y[0, cx, a] = flat
            Y[1, cx, a] = jnp.zeros((ROWS, cols), F32)
            put_operand(cx, a, flat)

    def put_operand(cx, a, flat):
        Vb[cx, a] = jnp.concatenate([flat, jnp.zeros((8, cols), F32)], axis=0).astype(BF16)

    loads[4].wait()
    for a in range(ZL):
        put_start(a, wave_lines(wave[a]))
        put_shift(a, pot[a])

    for c in setup[:2]:
        c.wait_recv()
    arrived = ini_r[...].astype(F32).reshape(LINES, 16, cols)
    put_start(ZL, (arrived[:, 0:8], arrived[:, 8:16]))
    put_shift(ZL, pot6[...])

    def put_projectors():
        for c in setup[2:] + metas:
            c.wait_recv()
        values = jnp.concatenate([pv[...], pvx[0], pvx[1]], axis=0).astype(F32)
        table = jnp.concatenate([meta[0], meta[n - 1], meta[1]], axis=0)
        cells = table[:, 64:65]
        group = lax.broadcasted_iota(jnp.int32, (56, 3 * PIECES), 1)
        parts = []
        for cell in range(6):
            masked = jnp.where(cells == float(cell), values, 0.0).astype(BF16)
            base = lax.dot_general(spread_t, masked, (((1,), (1,)), ((), ())), preferred_element_type=F32)
            low, high = base[0:56], base[384:440]
            layers = []
            for a in range(NL):
                here = jnp.where(group < PIECES, base[64 * a : 64 * a + 56], 0.0)
                if a == 0:
                    here = here + jnp.where(group >= 2 * PIECES, high, 0.0)
                if a == ZL:
                    here = here + jnp.where((group >= PIECES) & (group < 2 * PIECES), low, 0.0)
                layers.append(here)
            parts.append(layers)
        for a in range(NL):
            pair = []
            for cx in range(2):
                c0, c1, c2 = (parts[2 * cy + cx][a] for cy in range(3))
                whole = jnp.concatenate(
                    [c0[0:48], c0[48:56] + c1[0:8], c1[8:48], c1[48:56] + c2[0:8], c2[8:56]], axis=0
                )
                pair.append(whole.reshape(LINES, 8, 3 * PIECES))
            for cx, whole in enumerate(joined(*pair)):
                flat = whole.reshape(ROWS, 3 * PIECES)
                U[cx, a] = jnp.concatenate([flat, jnp.zeros((8, 3 * PIECES), F32)], axis=0).astype(BF16)

        count = coup.shape[1]
        number = lax.broadcasted_iota(jnp.int32, (1, count), 1).astype(F32)
        hot = jnp.where(table[:, 0:1] == number, 1.0, 0.0)
        every = jnp.where(meta[...].reshape(n * PIECES, 128)[:, 0:1] == number, 1.0, 0.0).astype(BF16)
        M[...] = lax.dot_general(
            hot.astype(BF16), every, (((1,), (1,)), ((), ())), preferred_element_type=F32
        ).astype(BF16)
        cpl[...] = jnp.broadcast_to(
            jnp.sum(hot * coup[...], axis=1, keepdims=True), (3 * PIECES, cols)
        )

    def add_cell(cx, cy, a, part):
        if cy == 0:
            acc[cx, a, 0:56] = part
        else:
            acc[cx, a, 48 * cy : 48 * cy + 8] += part[0:8]
            acc[cx, a, 48 * cy + 8 : 48 * cy + 56] = part[8:56]

    def both(a):
        return joined(
            acc[0, a].reshape(LINES, 8, cols), acc[1, a].reshape(LINES, 8, cols)
        )

    def step(k, last):
        cur = k % 2
        other = 1 - cur
        starts = isinstance(k, int) and k == 0
        factor = 1.0 if starts else 2.0
        back = 0.0 if starts else 1.0
        gain = factor * inv

        def operand(cx, cy):
            return Vb[cx, :, 48 * cy : 48 * cy + 64, :].reshape(KDIM, cols)

        total = jnp.zeros((PIECES, cols), F32)
        for cy in range(3):
            for cx in range(2):
                cell = 2 * cy + cx
                result = dot(L1[cell], operand(cx, cy))
                total = total + result[0:PIECES]
                factor_c = scale[cell]
                add_cell(cx, cy, 0, result[16:72] * factor_c)
                add_cell(cx, cy, ZL, result[72:128] * factor_c)
        coef[k, 0] = total.astype(BF16)
        coefs = [
            copy(coef.at[k, 0], coef.at[k, r], coef_ss.at[k, r], coef_rs.at[k, r], r) for r in range(1, n)
        ]
        for c in coefs:
            c.start()
        planes = []
        ends = [ZL] if last else [ZL, 0]
        for a in ends:
            pair = both(a)
            packed = jnp.concatenate(pair, axis=1).astype(BF16).reshape(LINES * 16, cols)
            if a == ZL:
                up_s[k] = packed
                c = copy(up_s.at[k], up_r.at[k], pl_ss.at[k, 0], pl_rs.at[k, 0], 1)
            else:
                dn_s[k] = packed
                c = copy(dn_s.at[k], dn_r.at[k], pl_ss.at[k, 1], pl_rs.at[k, 1], n - 1)
            c.start()
            planes.append(c)

        for cy in range(3):
            for cx in range(2):
                result = dot(L2[...], operand(cx, cy)) * scale[2 * cy + cx]
                for a in range(1, ZL):
                    add_cell(cx, cy, a, result[56 * (a - 1) : 56 * a])

        def partial(a):
            for cx, whole in enumerate(both(a)):
                shift = G[cx, a] * factor
                shift = jnp.concatenate([shift] * (cols // 128), axis=1)
                Y[other, cx, a] = (
                    whole.reshape(ROWS, cols) * gain + shift * Y[cur, cx, a] - back * Y[other, cx, a]
                )

        for a in range(ZL if last else NL):
            partial(a)

        if isinstance(k, int) and k == 0:
            put_projectors()
        for c in coefs:
            c.wait_recv()
        scaled = dot(M[...], coef[k].reshape(n * PIECES, cols)) * cpl[...]
        scaled = scaled.astype(BF16)

        def finish(a, extra):
            pair = []
            for cx in range(2):
                far = dot(U[cx, a], scaled)[0:ROWS]
                if extra is not None:
                    far = far + extra[cx].reshape(ROWS, cols)
                new = Y[other, cx, a] + gain * far
                if last:
                    pair.append(new.reshape(LINES, 8, cols))
                else:
                    Y[other, cx, a] = new
                    put_operand(cx, a, new)
            if last:
                out[a] = jnp.concatenate([pair[0][:, 0:7], pair[1][:, 1:7]], axis=1)

        for a in range(1, ZL):
            finish(a, None)
        for c in planes:
            c.wait_recv()
        got = up_r[k].astype(F32).reshape(LINES, 16, cols)
        finish(0, (got[:, 0:8], got[:, 8:16]))
        if not last:
            got = dn_r[k].astype(F32).reshape(LINES, 16, cols)
            finish(ZL, (got[:, 0:8], got[:, 8:16]))
        for c in coefs + planes:
            c.wait_send()

    step(0, False)

    @pl.loop(1, STEPS - 1)
    def _(k):
        step(k, False)

    step(STEPS - 1, True)
    for c in setup + metas:
        c.wait_send()


def local(n, wave, kinetic, cell_scale, potential, proj_values, piece_cell, piece_proj, coupling, center, halfwidth):
    cols = wave.shape[3]
    plane = (LINES * 16, cols)
    smem = pl.BlockSpec(memory_space=pltpu.SMEM)
    hbm = pl.BlockSpec(memory_space=pltpu.HBM)
    vmem = pl.BlockSpec(memory_space=pltpu.VMEM)
    dma = pltpu.SemaphoreType.DMA
    return pl.pallas_call(
        functools.partial(kernel, n),
        out_shape=jax.ShapeDtypeStruct(wave.shape, F32),
        in_specs=[smem] * 5 + [hbm] * 4 + [vmem],
        out_specs=vmem,
        scratch_shapes=[
            pltpu.VMEM(wave.shape, BF16),
            pltpu.VMEM(kinetic.shape, BF16),
            pltpu.VMEM((ZL, NXN, LINES), F32),
            pltpu.VMEM(proj_values.shape, BF16),
            dma((5,)),
            pltpu.VMEM((2, 2, NL, ROWS, cols), F32),
            pltpu.VMEM((2, NL, KROWS, cols), BF16),
            pltpu.VMEM((2, NL, ROWS, 128), F32),
            pltpu.VMEM((6, 128, KDIM), BF16),
            pltpu.VMEM((288, KDIM), BF16),
            pltpu.VMEM((2, NL, KROWS, 3 * PIECES), BF16),
            pltpu.VMEM((3 * PIECES, n * PIECES), BF16),
            pltpu.VMEM((2, NL, ROWS, cols), F32),
            pltpu.VMEM((NXN, LINES), F32),
            pltpu.VMEM((2,) + proj_values.shape, BF16),
            pltpu.VMEM((n, PIECES, 128), F32),
            pltpu.VMEM(plane, BF16),
            pltpu.VMEM(plane, BF16),
            pltpu.VMEM((STEPS,) + plane, BF16),
            pltpu.VMEM((STEPS,) + plane, BF16),
            pltpu.VMEM((STEPS - 1,) + plane, BF16),
            pltpu.VMEM((STEPS - 1,) + plane, BF16),
            pltpu.VMEM((STEPS, n, PIECES, cols), BF16),
            pltpu.VMEM((3 * PIECES, cols), F32),
            dma((n,)), dma((n,)), dma((4,)), dma((4,)),
            dma((STEPS, n)), dma((STEPS, n)), dma((STEPS, 2)), dma((STEPS, 2)),
        ],
        compiler_params=pltpu.CompilerParams(
            collective_id=0, has_side_effects=True, vmem_limit_bytes=64 * 1024 * 1024 - 65536
        ),
        name="filter",
    )(
        cell_scale, piece_cell, piece_proj, center, halfwidth,
        wave, kinetic, potential.transpose(0, 2, 1), proj_values, coupling[None, :],
    )


def solution(mesh):
    in_specs = (
        P("dom", None, None, "band"), P(), P("dom"), P("dom", None, None), P("dom", None),
        P("dom"), P("dom"), P(), P(), P(),
    )
    return jax.shard_map(
        functools.partial(local, mesh.shape["dom"]), mesh=mesh, in_specs=in_specs,
        out_specs=P("dom", None, None, "band"), check_vma=False,
    )
```

```python
import functools

import jax
import jax.numpy as jnp
from jax import lax
from jax.experimental import pallas as pl
from jax.experimental.pallas import tpu as pltpu
from jax.sharding import PartitionSpec as P

ZL = 6
NL = 7
LINES = 19
NXN = 13
ROWS = LINES * 8
KROWS = 160
KDIM = NL * 64
PIECES = 16
STEPS = 4
F32 = jnp.float32
BF16 = jnp.bfloat16


def dot(a, b):
    return jnp.dot(a, b, preferred_element_type=F32)


def joined(first, second):
    row = lax.broadcasted_iota(jnp.int32, first.shape, 1)
    moved_second = pltpu.roll(second, 6, 1)
    moved_first = pltpu.roll(first, 2, 1)
    return (
        first + jnp.where(row == 6, moved_second, 0.0),
        second + jnp.where(row == 0, moved_first, 0.0),
    )


def wave_lines(layer):
    layer = layer.astype(F32)
    empty = jnp.zeros((LINES, 1, layer.shape[2]), F32)
    return layer[:, 0:8], jnp.concatenate([layer[:, 6:NXN], empty], axis=1)


def kernel(
    n, scale, pc, pp, center, hw, wave_hbm, kin_hbm, pot_hbm, pv_hbm, coup, out,
    wave, kin, pot, pv, in_sem,
    Y, Vb, G, L1, L2, U, M, acc, pot6, pvx, meta, ini_s, ini_r,
    up_s, up_r, dn_s, dn_r, coef, cpl,
    meta_ss, meta_rs, set_ss, set_rs, coef_ss, coef_rs, pl_ss, pl_rs,
):
    me = lax.axis_index("dom")
    half, chip, core = n // 2, me // 2, me % 2
    cols = wave.shape[3]
    loads = [
        pltpu.make_async_copy(wave_hbm.at[0], wave.at[0], in_sem.at[0]),
        pltpu.make_async_copy(pot_hbm, pot, in_sem.at[1]),
        pltpu.make_async_copy(pv_hbm, pv, in_sem.at[2]),
        pltpu.make_async_copy(kin_hbm, kin, in_sem.at[3]),
        pltpu.make_async_copy(wave_hbm.at[1:ZL], wave.at[1:ZL], in_sem.at[4]),
    ]
    for c in loads:
        c.start()

    def to(offset):
        return {"dom": lax.rem(me + offset, n)}

    def copy(src, dst, ss, rs, offset):
        return pltpu.make_async_remote_copy(
            src_ref=src, dst_ref=dst, send_sem=ss, recv_sem=rs,
            device_id=to(offset), device_id_type=pl.DeviceIdType.MESH,
        )

    barrier = pltpu.get_barrier_semaphore()
    for r in range(1, n):
        pl.semaphore_signal(barrier, inc=1, device_id=to(r), device_id_type=pl.DeviceIdType.MESH)

    loads[0].wait()
    first, second = wave_lines(wave[0])
    ini_s[...] = jnp.concatenate([first, second], axis=1).astype(BF16).reshape(LINES * 16, cols)
    row = lax.broadcasted_iota(jnp.int32, (PIECES, 128), 0)
    lane = lax.broadcasted_iota(jnp.int32, (PIECES, 128), 1)
    table = jnp.zeros((PIECES, 128), jnp.int32)
    for i in range(PIECES):
        table = jnp.where(row == i, jnp.where(lane < 64, pp[i], pc[i]), table)
    meta[0] = table.astype(F32)

    loads[1].wait()
    loads[2].wait()
    pl.semaphore_wait(barrier, n - 1)
    setup = [
        copy(ini_s, ini_r, set_ss.at[0], set_rs.at[0], n - 1),
        copy(pot.at[0], pot6, set_ss.at[1], set_rs.at[1], n - 1),
        copy(pv, pvx.at[0], set_ss.at[2], set_rs.at[2], n - 1),
        copy(pv, pvx.at[1], set_ss.at[3], set_rs.at[3], 1),
    ]
    for c in setup:
        c.start()
    metas = [copy(meta.at[0], meta.at[r], meta_ss.at[r], meta_rs.at[r], r) for r in range(1, n)]
    for c in metas:
        c.start()

    def place(index):
        a, b, c = index // 64, (index // 8) % 8, index % 8
        return jnp.where((b < 7) & (c < 7), a * 49 + b * 7 + c, -1)

    loads[3].wait()
    nodes = kin.shape[0]
    spread = (
        lax.broadcasted_iota(jnp.int32, (nodes, KDIM), 0)
        == place(lax.broadcasted_iota(jnp.int32, (1, KDIM), 1))
    ).astype(F32).astype(BF16)
    spread_t = (
        lax.broadcasted_iota(jnp.int32, (KDIM, nodes), 1)
        == place(lax.broadcasted_iota(jnp.int32, (KDIM, 1), 0))
    ).astype(F32).astype(BF16)
    full = dot(spread_t, dot(kin[...], spread).astype(BF16))
    ends = jnp.concatenate([full[0:56], full[384:440]], axis=0)
    inner = [full[64 * a : 64 * a + 56] for a in range(1, ZL)]
    L2[...] = jnp.concatenate(inner + [jnp.zeros((8, KDIM), F32)], axis=0).astype(BF16)
    own = dot(pv[...], spread)
    own_cell = meta[0][:, 64:65]
    for cell in range(6):
        L1[cell] = jnp.concatenate([jnp.where(own_cell == float(cell), own, 0.0), ends], axis=0).astype(BF16)

    inv = 1.0 / hw[0]

    def put_shift(a, layer):
        layer = (layer - center[0]) * inv
        layer = jnp.concatenate([layer, jnp.zeros((3, LINES), F32)], axis=0)
        halves = (layer[0:8], pltpu.roll(layer, 10, 0)[0:8])
        for cx in range(2):
            for line in range(LINES):
                column = halves[cx][:, line : line + 1]
                G[cx, a, 8 * line : 8 * line + 8] = jnp.broadcast_to(column, (8, 128))

    def put_start(a, pair):
        for cx in range(2):
            flat = pair[cx].reshape(ROWS, cols)
            Y[0, cx, a] = flat
            Y[1, cx, a] = jnp.zeros((ROWS, cols), F32)
            put_operand(cx, a, flat)

    def put_operand(cx, a, flat):
        Vb[cx, a] = jnp.concatenate([flat, jnp.zeros((8, cols), F32)], axis=0).astype(BF16)

    loads[4].wait()
    for a in range(ZL):
        put_start(a, wave_lines(wave[a]))
        put_shift(a, pot[a])

    for c in setup[:2]:
        c.wait_recv()
    arrived = ini_r[...].astype(F32).reshape(LINES, 16, cols)
    put_start(ZL, (arrived[:, 0:8], arrived[:, 8:16]))
    put_shift(ZL, pot6[...])

    def put_projectors():
        for c in setup[2:] + metas:
            c.wait_recv()
        values = jnp.concatenate([pv[...], pvx[0], pvx[1]], axis=0).astype(F32)
        table = jnp.concatenate([meta[0], meta[n - 1], meta[1]], axis=0)
        cells = table[:, 64:65]
        group = lax.broadcasted_iota(jnp.int32, (56, 3 * PIECES), 1)
        parts = []
        for cell in range(6):
            masked = jnp.where(cells == float(cell), values, 0.0).astype(BF16)
            base = lax.dot_general(spread_t, masked, (((1,), (1,)), ((), ())), preferred_element_type=F32)
            low, high = base[0:56], base[384:440]
            layers = []
            for a in range(NL):
                here = jnp.where(group < PIECES, base[64 * a : 64 * a + 56], 0.0)
                if a == 0:
                    here = here + jnp.where(group >= 2 * PIECES, high, 0.0)
                if a == ZL:
                    here = here + jnp.where((group >= PIECES) & (group < 2 * PIECES), low, 0.0)
                layers.append(here)
            parts.append(layers)
        for a in range(NL):
            pair = []
            for cx in range(2):
                c0, c1, c2 = (parts[2 * cy + cx][a] for cy in range(3))
                whole = jnp.concatenate(
                    [c0[0:48], c0[48:56] + c1[0:8], c1[8:48], c1[48:56] + c2[0:8], c2[8:56]], axis=0
                )
                pair.append(whole.reshape(LINES, 8, 3 * PIECES))
            for cx, whole in enumerate(joined(*pair)):
                flat = whole.reshape(ROWS, 3 * PIECES)
                U[cx, a] = jnp.concatenate([flat, jnp.zeros((8, 3 * PIECES), F32)], axis=0).astype(BF16)

        count = coup.shape[1]
        number = lax.broadcasted_iota(jnp.int32, (1, count), 1).astype(F32)
        hot = jnp.where(table[:, 0:1] == number, 1.0, 0.0)
        ordered = [meta[lax.rem(me - 2 * c - p + n, n)] for p in range(2) for c in range(half)]
        ordered = jnp.concatenate(ordered, axis=0)
        every = jnp.where(ordered[:, 0:1] == number, 1.0, 0.0).astype(BF16)
        M[...] = lax.dot_general(
            hot.astype(BF16), every, (((1,), (1,)), ((), ())), preferred_element_type=F32
        ).astype(BF16)
        cpl[...] = jnp.broadcast_to(
            jnp.sum(hot * coup[...], axis=1, keepdims=True), (3 * PIECES, cols)
        )

    def add_cell(cx, cy, a, part):
        if cy == 0:
            acc[cx, a, 0:56] = part
        else:
            acc[cx, a, 48 * cy : 48 * cy + 8] += part[0:8]
            acc[cx, a, 48 * cy + 8 : 48 * cy + 56] = part[8:56]

    def both(a):
        return joined(
            acc[0, a].reshape(LINES, 8, cols), acc[1, a].reshape(LINES, 8, cols)
        )

    def step(k, last):
        cur = k % 2
        other = 1 - cur
        starts = isinstance(k, int) and k == 0
        factor = 1.0 if starts else 2.0
        back = 0.0 if starts else 1.0
        gain = factor * inv

        def operand(cx, cy):
            return Vb[cx, :, 48 * cy : 48 * cy + 64, :].reshape(KDIM, cols)

        total = jnp.zeros((PIECES, cols), F32)
        for cy in range(3):
            for cx in range(2):
                cell = 2 * cy + cx
                result = dot(L1[cell], operand(cx, cy))
                total = total + result[0:PIECES]
                factor_c = scale[cell]
                add_cell(cx, cy, 0, result[16:72] * factor_c)
                add_cell(cx, cy, ZL, result[72:128] * factor_c)
        coef[k, core, chip] = total.astype(BF16)
        coefs = [
            copy(coef.at[k, core, chip], coef.at[k, core, chip], coef_ss.at[k, r], coef_rs.at[k, r], 2 * r)
            for r in range(1, half)
        ]
        for c in coefs:
            c.start()
        planes = []
        ends = [ZL] if last else [ZL, 0]
        for a in ends:
            pair = both(a)
            packed = jnp.concatenate(pair, axis=1).astype(BF16).reshape(LINES * 16, cols)
            if a == ZL:
                up_s[k] = packed
                c = copy(up_s.at[k], up_r.at[k], pl_ss.at[k, 0], pl_rs.at[k, 0], 1)
            else:
                dn_s[k] = packed
                c = copy(dn_s.at[k], dn_r.at[k], pl_ss.at[k, 1], pl_rs.at[k, 1], n - 1)
            c.start()
            planes.append(c)

        for cy in range(3):
            for cx in range(2):
                result = dot(L2[...], operand(cx, cy)) * scale[2 * cy + cx]
                for a in range(1, ZL):
                    add_cell(cx, cy, a, result[56 * (a - 1) : 56 * a])

        for c in coefs:
            c.wait_recv()
        handed = copy(coef.at[k, core], coef.at[k, core], coef_ss.at[k, 0], coef_rs.at[k, 0], 1 + core * (n - 2))
        handed.start()

        def partial(a):
            for cx, whole in enumerate(both(a)):
                shift = G[cx, a] * factor
                shift = jnp.concatenate([shift] * (cols // 128), axis=1)
                Y[other, cx, a] = (
                    whole.reshape(ROWS, cols) * gain + shift * Y[cur, cx, a] - back * Y[other, cx, a]
                )

        for a in range(ZL if last else NL):
            partial(a)

        if isinstance(k, int) and k == 0:
            put_projectors()
        handed.wait_recv()
        scaled = dot(M[...], coef[k].reshape(n * PIECES, cols)) * cpl[...]
        scaled = scaled.astype(BF16)

        def finish(a, extra):
            pair = []
            for cx in range(2):
                far = dot(U[cx, a], scaled)[0:ROWS]
                if extra is not None:
                    far = far + extra[cx].reshape(ROWS, cols)
                new = Y[other, cx, a] + gain * far
                if last:
                    pair.append(new.reshape(LINES, 8, cols))
                else:
                    Y[other, cx, a] = new
                    put_operand(cx, a, new)
            if last:
                out[a] = jnp.concatenate([pair[0][:, 0:7], pair[1][:, 1:7]], axis=1)

        for a in range(1, ZL):
            finish(a, None)
        for c in planes:
            c.wait_recv()
        got = up_r[k].astype(F32).reshape(LINES, 16, cols)
        finish(0, (got[:, 0:8], got[:, 8:16]))
        if not last:
            got = dn_r[k].astype(F32).reshape(LINES, 16, cols)
            finish(ZL, (got[:, 0:8], got[:, 8:16]))
        for c in coefs + [handed] + planes:
            c.wait_send()

    step(0, False)

    @pl.loop(1, STEPS - 1)
    def _(k):
        step(k, False)

    step(STEPS - 1, True)
    for c in setup + metas:
        c.wait_send()


def local(n, wave, kinetic, cell_scale, potential, proj_values, piece_cell, piece_proj, coupling, center, halfwidth):
    cols = wave.shape[3]
    plane = (LINES * 16, cols)
    smem = pl.BlockSpec(memory_space=pltpu.SMEM)
    hbm = pl.BlockSpec(memory_space=pltpu.HBM)
    vmem = pl.BlockSpec(memory_space=pltpu.VMEM)
    dma = pltpu.SemaphoreType.DMA
    return pl.pallas_call(
        functools.partial(kernel, n),
        out_shape=jax.ShapeDtypeStruct(wave.shape, F32),
        in_specs=[smem] * 5 + [hbm] * 4 + [vmem],
        out_specs=vmem,
        scratch_shapes=[
            pltpu.VMEM(wave.shape, BF16),
            pltpu.VMEM(kinetic.shape, BF16),
            pltpu.VMEM((ZL, NXN, LINES), F32),
            pltpu.VMEM(proj_values.shape, BF16),
            dma((5,)),
            pltpu.VMEM((2, 2, NL, ROWS, cols), F32),
            pltpu.VMEM((2, NL, KROWS, cols), BF16),
            pltpu.VMEM((2, NL, ROWS, 128), F32),
            pltpu.VMEM((6, 128, KDIM), BF16),
            pltpu.VMEM((288, KDIM), BF16),
            pltpu.VMEM((2, NL, KROWS, 3 * PIECES), BF16),
            pltpu.VMEM((3 * PIECES, n * PIECES), BF16),
            pltpu.VMEM((2, NL, ROWS, cols), F32),
            pltpu.VMEM((NXN, LINES), F32),
            pltpu.VMEM((2,) + proj_values.shape, BF16),
            pltpu.VMEM((n, PIECES, 128), F32),
            pltpu.VMEM(plane, BF16),
            pltpu.VMEM(plane, BF16),
            pltpu.VMEM((STEPS,) + plane, BF16),
            pltpu.VMEM((STEPS,) + plane, BF16),
            pltpu.VMEM((STEPS - 1,) + plane, BF16),
            pltpu.VMEM((STEPS - 1,) + plane, BF16),
            pltpu.VMEM((STEPS, 2, n // 2, PIECES, cols), BF16),
            pltpu.VMEM((3 * PIECES, cols), F32),
            dma((n,)), dma((n,)), dma((4,)), dma((4,)),
            dma((STEPS, n // 2)), dma((STEPS, n // 2)), dma((STEPS, 2)), dma((STEPS, 2)),
        ],
        compiler_params=pltpu.CompilerParams(
            collective_id=0, has_side_effects=True, vmem_limit_bytes=64 * 1024 * 1024 - 65536
        ),
        name="filter",
    )(
        cell_scale, piece_cell, piece_proj, center, halfwidth,
        wave, kinetic, potential.transpose(0, 2, 1), proj_values, coupling[None, :],
    )


def solution(mesh):
    in_specs = (
        P("dom", None, None, "band"), P(), P("dom"), P("dom", None, None), P("dom", None),
        P("dom"), P("dom"), P(), P(), P(),
    )
    return jax.shard_map(
        functools.partial(local, mesh.shape["dom"]), mesh=mesh, in_specs=in_specs,
        out_specs=P("dom", None, None, "band"), check_vma=False,
    )
```

```python
import functools

import jax
import jax.numpy as jnp
from jax import lax
from jax.experimental import pallas as pl
from jax.experimental.pallas import tpu as pltpu
from jax.sharding import PartitionSpec as P

ZL = 6
NL = 7
LINES = 19
NXN = 13
ROWS = LINES * 8
KROWS = 160
KDIM = NL * 64
PIECES = 16
STEPS = 4
F32 = jnp.float32
BF16 = jnp.bfloat16


def dot(a, b):
    return jnp.dot(a, b, preferred_element_type=F32)


def joined(first, second):
    row = lax.broadcasted_iota(jnp.int32, first.shape, 1)
    moved_second = pltpu.roll(second, 6, 1)
    moved_first = pltpu.roll(first, 2, 1)
    return (
        first + jnp.where(row == 6, moved_second, 0.0),
        second + jnp.where(row == 0, moved_first, 0.0),
    )


def wave_lines(layer):
    layer = layer.astype(F32)
    empty = jnp.zeros((LINES, 1, layer.shape[2]), F32)
    return layer[:, 0:8], jnp.concatenate([layer[:, 6:NXN], empty], axis=1)


SPARE = (7, 8, 15)


def pack(pair):
    whole = jnp.concatenate(pair, axis=1)
    cols = whole.shape[2]
    packed = whole[0:16]
    row = lax.broadcasted_iota(jnp.int32, packed.shape, 1)
    for i, spare in enumerate(SPARE):
        line = whole[16 + i]
        nodes = jnp.concatenate([line[0:7], line[9:15], jnp.zeros((3, cols), F32)], axis=0)
        packed = jnp.where(row == spare, jnp.broadcast_to(nodes[:, None, :], packed.shape), packed)
    return packed.astype(BF16).reshape(256, cols)


def unpack(packed):
    cols = packed.shape[1]
    whole = packed.astype(F32).reshape(16, 16, cols)
    first, second = whole[:, 0:8], whole[:, 8:16]
    row = lax.broadcasted_iota(jnp.int32, first.shape, 1)
    firsts = [first]
    seconds = [jnp.where(row == 0, pltpu.roll(first, 2, 1), second)]
    for spare in SPARE:
        nodes = whole[:, spare]
        firsts.append(nodes[0:8][None])
        seconds.append(jnp.concatenate([nodes[6:13], jnp.zeros((1, cols), F32)], axis=0)[None])
    return jnp.concatenate(firsts, axis=0), jnp.concatenate(seconds, axis=0)


def kernel(
    n, scale, pc, pp, center, hw, wave_hbm, kin_hbm, pot_hbm, pv_hbm, coup, out,
    wave, kin, pot, pv, in_sem,
    Y, Vb, G, L1, L2, U, M, acc, pot6, pvx, meta, ini_s, ini_r,
    up_s, up_r, dn_s, dn_r, coef, cpl,
    meta_ss, meta_rs, set_ss, set_rs, coef_ss, coef_rs, pl_ss, pl_rs,
):
    me = lax.axis_index("dom")
    half, chip, core = n // 2, me // 2, me % 2
    cols = wave.shape[3]
    loads = [
        pltpu.make_async_copy(wave_hbm.at[0], wave.at[0], in_sem.at[0]),
        pltpu.make_async_copy(pot_hbm, pot, in_sem.at[1]),
        pltpu.make_async_copy(pv_hbm, pv, in_sem.at[2]),
        pltpu.make_async_copy(kin_hbm, kin, in_sem.at[3]),
        pltpu.make_async_copy(wave_hbm.at[1:ZL], wave.at[1:ZL], in_sem.at[4]),
    ]
    for c in loads:
        c.start()

    def to(offset):
        return {"dom": lax.rem(me + offset, n)}

    def copy(src, dst, ss, rs, offset):
        return pltpu.make_async_remote_copy(
            src_ref=src, dst_ref=dst, send_sem=ss, recv_sem=rs,
            device_id=to(offset), device_id_type=pl.DeviceIdType.MESH,
        )

    barrier = pltpu.get_barrier_semaphore()
    for r in range(1, n):
        pl.semaphore_signal(barrier, inc=1, device_id=to(r), device_id_type=pl.DeviceIdType.MESH)

    loads[0].wait()
    ini_s[...] = pack(wave_lines(wave[0]))
    row = lax.broadcasted_iota(jnp.int32, (PIECES, 128), 0)
    lane = lax.broadcasted_iota(jnp.int32, (PIECES, 128), 1)
    table = jnp.zeros((PIECES, 128), jnp.int32)
    for i in range(PIECES):
        table = jnp.where(row == i, jnp.where(lane < 64, pp[i], pc[i]), table)
    meta[0] = table.astype(F32)

    loads[1].wait()
    loads[2].wait()
    pl.semaphore_wait(barrier, n - 1)
    setup = [
        copy(ini_s, ini_r, set_ss.at[0], set_rs.at[0], n - 1),
        copy(pot.at[0], pot6, set_ss.at[1], set_rs.at[1], n - 1),
        copy(pv, pvx.at[0], set_ss.at[2], set_rs.at[2], n - 1),
        copy(pv, pvx.at[1], set_ss.at[3], set_rs.at[3], 1),
    ]
    for c in setup:
        c.start()
    metas = [copy(meta.at[0], meta.at[r], meta_ss.at[r], meta_rs.at[r], r) for r in range(1, n)]
    for c in metas:
        c.start()

    def place(index):
        a, b, c = index // 64, (index // 8) % 8, index % 8
        return jnp.where((b < 7) & (c < 7), a * 49 + b * 7 + c, -1)

    loads[3].wait()
    nodes = kin.shape[0]
    spread = (
        lax.broadcasted_iota(jnp.int32, (nodes, KDIM), 0)
        == place(lax.broadcasted_iota(jnp.int32, (1, KDIM), 1))
    ).astype(F32).astype(BF16)
    spread_t = (
        lax.broadcasted_iota(jnp.int32, (KDIM, nodes), 1)
        == place(lax.broadcasted_iota(jnp.int32, (KDIM, 1), 0))
    ).astype(F32).astype(BF16)
    full = dot(spread_t, dot(kin[...], spread).astype(BF16))
    ends = jnp.concatenate([full[0:56], full[384:440]], axis=0)
    inner = [full[64 * a : 64 * a + 56] for a in range(1, ZL)]
    L2[...] = jnp.concatenate(inner + [jnp.zeros((8, KDIM), F32)], axis=0).astype(BF16)
    own = dot(pv[...], spread)
    own_cell = meta[0][:, 64:65]
    for cell in range(6):
        L1[cell] = jnp.concatenate([jnp.where(own_cell == float(cell), own, 0.0), ends], axis=0).astype(BF16)

    inv = 1.0 / hw[0]

    def put_shift(a, layer):
        layer = (layer - center[0]) * inv
        layer = jnp.concatenate([layer, jnp.zeros((3, LINES), F32)], axis=0)
        halves = (layer[0:8], pltpu.roll(layer, 10, 0)[0:8])
        for cx in range(2):
            for line in range(LINES):
                column = halves[cx][:, line : line + 1]
                G[cx, a, 8 * line : 8 * line + 8] = jnp.broadcast_to(column, (8, 128))

    def put_start(a, pair):
        for cx in range(2):
            flat = pair[cx].reshape(ROWS, cols)
            Y[0, cx, a] = flat
            Y[1, cx, a] = jnp.zeros((ROWS, cols), F32)
            put_operand(cx, a, flat)

    def put_operand(cx, a, flat):
        Vb[cx, a] = jnp.concatenate([flat, jnp.zeros((8, cols), F32)], axis=0).astype(BF16)

    loads[4].wait()
    for a in range(ZL):
        put_start(a, wave_lines(wave[a]))
        put_shift(a, pot[a])

    for c in setup[:2]:
        c.wait_recv()
    put_start(ZL, unpack(ini_r[...]))
    put_shift(ZL, pot6[...])

    def put_projectors():
        for c in setup[2:] + metas:
            c.wait_recv()
        values = jnp.concatenate([pv[...], pvx[0], pvx[1]], axis=0).astype(F32)
        table = jnp.concatenate([meta[0], meta[n - 1], meta[1]], axis=0)
        cells = table[:, 64:65]
        group = lax.broadcasted_iota(jnp.int32, (56, 3 * PIECES), 1)
        parts = []
        for cell in range(6):
            masked = jnp.where(cells == float(cell), values, 0.0).astype(BF16)
            base = lax.dot_general(spread_t, masked, (((1,), (1,)), ((), ())), preferred_element_type=F32)
            low, high = base[0:56], base[384:440]
            layers = []
            for a in range(NL):
                here = jnp.where(group < PIECES, base[64 * a : 64 * a + 56], 0.0)
                if a == 0:
                    here = here + jnp.where(group >= 2 * PIECES, high, 0.0)
                if a == ZL:
                    here = here + jnp.where((group >= PIECES) & (group < 2 * PIECES), low, 0.0)
                layers.append(here)
            parts.append(layers)
        for a in range(NL):
            pair = []
            for cx in range(2):
                c0, c1, c2 = (parts[2 * cy + cx][a] for cy in range(3))
                whole = jnp.concatenate(
                    [c0[0:48], c0[48:56] + c1[0:8], c1[8:48], c1[48:56] + c2[0:8], c2[8:56]], axis=0
                )
                pair.append(whole.reshape(LINES, 8, 3 * PIECES))
            for cx, whole in enumerate(joined(*pair)):
                flat = whole.reshape(ROWS, 3 * PIECES)
                U[cx, a] = jnp.concatenate([flat, jnp.zeros((8, 3 * PIECES), F32)], axis=0).astype(BF16)

        count = coup.shape[1]
        number = lax.broadcasted_iota(jnp.int32, (1, count), 1).astype(F32)
        hot = jnp.where(table[:, 0:1] == number, 1.0, 0.0)
        ordered = [meta[lax.rem(me - 2 * c - p + n, n)] for p in range(2) for c in range(half)]
        ordered = jnp.concatenate(ordered, axis=0)
        every = jnp.where(ordered[:, 0:1] == number, 1.0, 0.0).astype(BF16)
        M[...] = lax.dot_general(
            hot.astype(BF16), every, (((1,), (1,)), ((), ())), preferred_element_type=F32
        ).astype(BF16)
        cpl[...] = jnp.broadcast_to(
            jnp.sum(hot * coup[...], axis=1, keepdims=True), (3 * PIECES, cols)
        )

    def add_cell(cx, cy, a, part):
        if cy == 0:
            acc[cx, a, 0:56] = part
        else:
            acc[cx, a, 48 * cy : 48 * cy + 8] += part[0:8]
            acc[cx, a, 48 * cy + 8 : 48 * cy + 56] = part[8:56]

    def both(a):
        return joined(
            acc[0, a].reshape(LINES, 8, cols), acc[1, a].reshape(LINES, 8, cols)
        )

    def step(k, last):
        cur = k % 2
        other = 1 - cur
        starts = isinstance(k, int) and k == 0
        factor = 1.0 if starts else 2.0
        back = 0.0 if starts else 1.0
        gain = factor * inv

        def operand(cx, cy):
            return Vb[cx, :, 48 * cy : 48 * cy + 64, :].reshape(KDIM, cols)

        total = jnp.zeros((PIECES, cols), F32)
        for cy in range(3):
            for cx in range(2):
                cell = 2 * cy + cx
                result = dot(L1[cell], operand(cx, cy))
                total = total + result[0:PIECES]
                factor_c = scale[cell]
                add_cell(cx, cy, 0, result[16:72] * factor_c)
                add_cell(cx, cy, ZL, result[72:128] * factor_c)
        coef[k, core, chip] = total.astype(BF16)
        coefs = [
            copy(coef.at[k, core, chip], coef.at[k, core, chip], coef_ss.at[k, r], coef_rs.at[k, r], 2 * r)
            for r in range(1, half)
        ]
        for c in coefs:
            c.start()
        planes = []
        ends = [ZL] if last else [ZL, 0]
        for a in ends:
            pair = both(a)
            packed = pack(pair)
            if a == ZL:
                up_s[k] = packed
                c = copy(up_s.at[k], up_r.at[k], pl_ss.at[k, 0], pl_rs.at[k, 0], 1)
            else:
                dn_s[k] = packed
                c = copy(dn_s.at[k], dn_r.at[k], pl_ss.at[k, 1], pl_rs.at[k, 1], n - 1)
            c.start()
            planes.append(c)

        for cy in range(3):
            for cx in range(2):
                result = dot(L2[...], operand(cx, cy)) * scale[2 * cy + cx]
                for a in range(1, ZL):
                    add_cell(cx, cy, a, result[56 * (a - 1) : 56 * a])

        for c in coefs:
            c.wait_recv()
        handed = copy(coef.at[k, core], coef.at[k, core], coef_ss.at[k, 0], coef_rs.at[k, 0], 1 + core * (n - 2))
        handed.start()

        def partial(a):
            for cx, whole in enumerate(both(a)):
                shift = G[cx, a] * factor
                shift = jnp.concatenate([shift] * (cols // 128), axis=1)
                Y[other, cx, a] = (
                    whole.reshape(ROWS, cols) * gain + shift * Y[cur, cx, a] - back * Y[other, cx, a]
                )

        for a in range(ZL if last else NL):
            partial(a)

        if isinstance(k, int) and k == 0:
            put_projectors()
        handed.wait_recv()
        scaled = dot(M[...], coef[k].reshape(n * PIECES, cols)) * cpl[...]
        scaled = scaled.astype(BF16)

        def finish(a, extra):
            pair = []
            for cx in range(2):
                far = dot(U[cx, a], scaled)[0:ROWS]
                if extra is not None:
                    far = far + extra[cx].reshape(ROWS, cols)
                new = Y[other, cx, a] + gain * far
                if last:
                    pair.append(new.reshape(LINES, 8, cols))
                else:
                    Y[other, cx, a] = new
                    put_operand(cx, a, new)
            if last:
                out[a] = jnp.concatenate([pair[0][:, 0:7], pair[1][:, 1:7]], axis=1)

        for a in range(1, ZL):
            finish(a, None)
        for c in planes:
            c.wait_recv()
        finish(0, unpack(up_r[k]))
        if not last:
            finish(ZL, unpack(dn_r[k]))
        for c in coefs + [handed] + planes:
            c.wait_send()

    step(0, False)

    @pl.loop(1, STEPS - 1)
    def _(k):
        step(k, False)

    step(STEPS - 1, True)
    for c in setup + metas:
        c.wait_send()


def local(n, wave, kinetic, cell_scale, potential, proj_values, piece_cell, piece_proj, coupling, center, halfwidth):
    cols = wave.shape[3]
    plane = (256, cols)
    smem = pl.BlockSpec(memory_space=pltpu.SMEM)
    hbm = pl.BlockSpec(memory_space=pltpu.HBM)
    vmem = pl.BlockSpec(memory_space=pltpu.VMEM)
    dma = pltpu.SemaphoreType.DMA
    return pl.pallas_call(
        functools.partial(kernel, n),
        out_shape=jax.ShapeDtypeStruct(wave.shape, F32),
        in_specs=[smem] * 5 + [hbm] * 4 + [vmem],
        out_specs=vmem,
        scratch_shapes=[
            pltpu.VMEM(wave.shape, BF16),
            pltpu.VMEM(kinetic.shape, BF16),
            pltpu.VMEM((ZL, NXN, LINES), F32),
            pltpu.VMEM(proj_values.shape, BF16),
            dma((5,)),
            pltpu.VMEM((2, 2, NL, ROWS, cols), F32),
            pltpu.VMEM((2, NL, KROWS, cols), BF16),
            pltpu.VMEM((2, NL, ROWS, 128), F32),
            pltpu.VMEM((6, 128, KDIM), BF16),
            pltpu.VMEM((288, KDIM), BF16),
            pltpu.VMEM((2, NL, KROWS, 3 * PIECES), BF16),
            pltpu.VMEM((3 * PIECES, n * PIECES), BF16),
            pltpu.VMEM((2, NL, ROWS, cols), F32),
            pltpu.VMEM((NXN, LINES), F32),
            pltpu.VMEM((2,) + proj_values.shape, BF16),
            pltpu.VMEM((n, PIECES, 128), F32),
            pltpu.VMEM(plane, BF16),
            pltpu.VMEM(plane, BF16),
            pltpu.VMEM((STEPS,) + plane, BF16),
            pltpu.VMEM((STEPS,) + plane, BF16),
            pltpu.VMEM((STEPS - 1,) + plane, BF16),
            pltpu.VMEM((STEPS - 1,) + plane, BF16),
            pltpu.VMEM((STEPS, 2, n // 2, PIECES, cols), BF16),
            pltpu.VMEM((3 * PIECES, cols), F32),
            dma((n,)), dma((n,)), dma((4,)), dma((4,)),
            dma((STEPS, n // 2)), dma((STEPS, n // 2)), dma((STEPS, 2)), dma((STEPS, 2)),
        ],
        compiler_params=pltpu.CompilerParams(
            collective_id=0, has_side_effects=True, vmem_limit_bytes=64 * 1024 * 1024 - 65536
        ),
        name="filter",
    )(
        cell_scale, piece_cell, piece_proj, center, halfwidth,
        wave, kinetic, potential.transpose(0, 2, 1), proj_values, coupling[None, :],
    )


def solution(mesh):
    in_specs = (
        P("dom", None, None, "band"), P(), P("dom"), P("dom", None, None), P("dom", None),
        P("dom"), P("dom"), P(), P(), P(),
    )
    return jax.shard_map(
        functools.partial(local, mesh.shape["dom"]), mesh=mesh, in_specs=in_specs,
        out_specs=P("dom", None, None, "band"), check_vma=False,
    )
```
